256 devices in a mesh: prompt: 16 (over z, core), leaf: 16 (over y, x).
Axes of the slice: x: 4, y: 4, z: 8, core: 2. Of those that a mesh axis runs over, the one named last changes fastest.
Arguments:
- queries: bfloat16 [256, 2, 128, 5120], P(('prompt', 'leaf')), parts along dimension 0, may hold values from -6 to 6
- keys: bfloat16 [256, 2, 128, 1024], P(('prompt', 'leaf')), parts along dimension 0, may hold values from -6 to 6
- values: bfloat16 [256, 2, 128, 1024], P(('prompt', 'leaf')), parts along dimension 0, may hold values from -6 to 6
- out_grad: bfloat16 [256, 2, 128, 5120], P(('prompt', 'leaf')), parts along dimension 0, may hold values from -6 to 6
- seg_lengths: int32 [256, 2], P('prompt'), parts along dimension 0, may hold values from 64 to 128, as said below
Outputs:
- grad_queries: bfloat16 [256, 2, 128, 5120], P(('prompt', 'leaf')), parts along dimension 0
- grad_keys: bfloat16 [256, 2, 128, 1024], P(('prompt', 'leaf')), parts along dimension 0
- grad_values: bfloat16 [256, 2, 128, 1024], P(('prompt', 'leaf')), parts along dimension 0
The draws below stay inside these ranges and needn't reach their ends.
There are 16 independent parts, one for each index of `prompt`. The reference program is written for one: setup_inputs(seed, part) draws one part's arguments, and reference() takes and returns one part's arrays. A program takes and returns all parts, laid end to end along the dimension named above; each array names one. Nothing has to cross between parts.
Inputs may be any that keep to these rules, and one draw needn't show every extreme that they name: `seg_lengths`: the number of leading slots of a segment that hold tokens; some segment of each prompt holds 128.
All inputs are finite; a program needn't handle non-finite values.
Results may differ from the reference program's by a relative error of at most 0.012.
Values may be sent and summed in bfloat16 or wider, within the bound.
No kernel may reach another device: no remote copies, remote signals or barrier semaphores. Data moves between devices by JAX's collectives and lax.ppermute only.
A program may use at most 128 MiB of HBM per device.

```python
import math
import jax
import jax.numpy as jnp
import numpy as np
from jax import lax

QUERY_HEADS = 40
KEY_VALUE_HEADS = 8
HEAD_WIDTH = 128
SEGMENT_SLOTS = 128
QUERY_PER_KEY = 5
BRANCH_DEPTH = 4
N_LEAF = 16


def draw_queries(key, part):
    key = jax.random.fold_in(key, 11)
    sampled_picks = jax.random.truncated_normal(key, -4.0, 4.0, (N_LEAF, 2, SEGMENT_SLOTS, QUERY_HEADS, HEAD_WIDTH), jnp.float32)
    return sampled_picks.reshape(N_LEAF, 2, SEGMENT_SLOTS, QUERY_HEADS * HEAD_WIDTH).astype(jnp.bfloat16)


def draw_keys(key, part):
    key = jax.random.fold_in(key, 12)
    sampled_picks = jax.random.truncated_normal(key, -4.0, 4.0, (N_LEAF, 2, SEGMENT_SLOTS, KEY_VALUE_HEADS, HEAD_WIDTH), jnp.float32)
    return sampled_picks.reshape(N_LEAF, 2, SEGMENT_SLOTS, KEY_VALUE_HEADS * HEAD_WIDTH).astype(jnp.bfloat16)


def draw_seg_lengths(key, part):
    key = jax.random.fold_in(key, 13)
    first, second = jax.random.split(key)
    lengths = jax.random.randint(first, (N_LEAF, 2), SEGMENT_SLOTS // 2, SEGMENT_SLOTS + 1)
    chosen = jax.random.randint(second, (), 0, 2 * N_LEAF)
    flat_lengths = lengths.reshape(-1)
    flat_lengths = jnp.where(jnp.arange(2 * N_LEAF) == chosen, SEGMENT_SLOTS, flat_lengths)
    return flat_lengths.reshape(N_LEAF, 2).astype(jnp.int32)


def shard_levels(key, shape, cuts, least, largest):
    loudness, own = 1.0, jax.random.fold_in(key, 6)
    for dim, blocks in cuts:
        draws = jnp.exp(jax.random.uniform(jax.random.fold_in(own, dim), (blocks,), jnp.float32, least / len(cuts), largest / len(cuts)))
        loudness = loudness * jnp.repeat(draws, shape[dim] // blocks).reshape([-1 if axis == dim else 1 for axis in range(len(shape))])
    return loudness


def noise(rng, extent, width, most, pieces=(), kind=jnp.bfloat16):
    drawn = jax.random.normal(rng, extent, jnp.float32) * width
    if len(pieces) > 0:
        drawn = shard_levels(rng, extent, pieces, -0.22, 0.18) * drawn
    return jnp.clip(drawn, min=-most, max=most).astype(kind)


def setup_inputs(seed: int = 0, part: int = 0) -> dict:
    seeds = jax.random.split(jax.random.key(seed), 6)
    part_splits = jax.random.split(jax.random.fold_in(seeds[5], part), 6)
    return {
        "queries": draw_queries(jax.random.fold_in(jax.random.fold_in(seeds[5], part), 71), part),
        "keys": draw_keys(jax.random.fold_in(jax.random.fold_in(seeds[5], part), 71), part),
        "values": noise(part_splits[2], (N_LEAF, 2, SEGMENT_SLOTS, KEY_VALUE_HEADS * HEAD_WIDTH), 1.0, 6.0, ((0, 16),)),
        "out_grad": noise(part_splits[3], (N_LEAF, 2, SEGMENT_SLOTS, QUERY_HEADS * HEAD_WIDTH), 1.0, 6.0, ((0, 16),)),
        "seg_lengths": draw_seg_lengths(jax.random.fold_in(jax.random.fold_in(seeds[5], part), 71), part),
    }


def context_tables():
    owners = np.zeros((N_LEAF, BRANCH_DEPTH + 2), np.int32)
    slot_index = np.zeros((N_LEAF, BRANCH_DEPTH + 2), np.int32)
    places = np.zeros((N_LEAF,), np.int32)
    for leaf_index in range(N_LEAF):
        for position in range(1, BRANCH_DEPTH + 1):
            span_width = 2 ** (BRANCH_DEPTH - position + 1)
            owners[leaf_index, position] = leaf_index // span_width * span_width + span_width // 2
            if owners[leaf_index, position] == leaf_index:
                places[leaf_index] = position
        owners[leaf_index, BRANCH_DEPTH + 1] = leaf_index
        slot_index[leaf_index, BRANCH_DEPTH + 1] = 1
    return (owners, slot_index, places)

def allowed_mask(ctx_lengths, own_lengths, inner_place, seg_len):
    seg_total = ctx_lengths.shape[0]
    key_place = jnp.repeat(jnp.arange(seg_total, dtype=jnp.int32), seg_len)
    key_slot = jnp.tile(jnp.arange(seg_len, dtype=jnp.int32), seg_total)
    key_live = key_slot < jnp.repeat(ctx_lengths, seg_len)
    query_slot = jnp.tile(jnp.arange(seg_len, dtype=jnp.int32), 2)
    query_place = jnp.concatenate([jnp.zeros((seg_len,), jnp.int32) + inner_place, jnp.full((seg_len,), seg_total - 1, jnp.int32)])
    earlier = key_place[None, :] < query_place[:, None]
    causal = (key_place[None, :] == query_place[:, None]) & (key_slot[None, :] <= query_slot[:, None])
    allowed = key_live[None, :] & (earlier | causal)
    query_live = query_slot < jnp.repeat(own_lengths, seg_len)
    return (allowed, query_live)

def attend_backward(local_query_rows, context_key_rows, context_value_rows, own_grad, allowed, query_live):
    total_row_number = local_query_rows.shape[0]
    score_scale = 1.0 / math.sqrt(HEAD_WIDTH)
    running_gradient = jnp.where(query_live[:, None], own_grad, jnp.zeros_like(own_grad))
    query_head_rows = local_query_rows.reshape(total_row_number, KEY_VALUE_HEADS, QUERY_PER_KEY, HEAD_WIDTH).transpose(1, 0, 2, 3)
    head_gradient_rows = running_gradient.reshape(total_row_number, KEY_VALUE_HEADS, QUERY_PER_KEY, HEAD_WIDTH).transpose(1, 0, 2, 3)
    key_head_rows = context_key_rows.reshape(-1, KEY_VALUE_HEADS, HEAD_WIDTH).transpose(1, 0, 2)
    value_head_rows = context_value_rows.reshape(-1, KEY_VALUE_HEADS, HEAD_WIDTH).transpose(1, 0, 2)

    def per_group(operands):
        query_group, key_group, value_group, grad_group = operands
        query_wide = query_group.astype(jnp.float32)
        key_wide = key_group.astype(jnp.float32)
        value_wide = value_group.astype(jnp.float32)
        grad_wide = grad_group.astype(jnp.float32)
        scores = jnp.einsum('rgd,cd->grc', query_wide, key_wide) * score_scale
        scores = jnp.where(allowed[None], scores, -jnp.inf)
        highest = lax.optimization_barrier(jnp.max(scores, axis=-1, keepdims=True))
        exponent = jnp.exp(scores - highest)
        weights = exponent / lax.optimization_barrier(jnp.sum(exponent, axis=-1, keepdims=True))
        weights_half = lax.optimization_barrier(weights.astype(jnp.bfloat16))
        weights_back = weights_half.astype(jnp.float32)
        output = jnp.einsum('grc,cd->rgd', weights_back, value_wide)
        row_delta = jnp.transpose(lax.optimization_barrier(jnp.sum(grad_wide * output, axis=-1)))
        weight_grad = jnp.einsum('rgd,cd->grc', grad_wide, value_wide)
        score_grad = weights * (weight_grad - row_delta[:, :, None])
        score_half = lax.optimization_barrier(score_grad.astype(jnp.bfloat16))
        score_back = score_half.astype(jnp.float32)
        query_gradient_block = jnp.einsum('grc,cd->rgd', score_back, key_wide) * score_scale
        key_gradient_block = jnp.einsum('grc,rgd->cd', score_back, query_wide) * score_scale
        value_gradient_block = jnp.einsum('grc,rgd->cd', weights_back, grad_wide)
        return (query_gradient_block, key_gradient_block, value_gradient_block)
    query_gradient_block, key_gradient_block, value_gradient_block = lax.map(per_group, (query_head_rows, key_head_rows, value_head_rows, head_gradient_rows))
    query_gradient_block = query_gradient_block.transpose(1, 0, 2, 3).reshape(total_row_number, QUERY_HEADS * HEAD_WIDTH)
    key_gradient_block = key_gradient_block.transpose(1, 0, 2).reshape(-1, KEY_VALUE_HEADS * HEAD_WIDTH)
    value_gradient_block = value_gradient_block.transpose(1, 0, 2).reshape(-1, KEY_VALUE_HEADS * HEAD_WIDTH)
    return (query_gradient_block, key_gradient_block, value_gradient_block)

def reference(queries, keys, values, out_grad, seg_lengths):
    owners, slot_index, places = context_tables()

    def per_device(operands):
        leaf_index, keeper_row, position_row, inner_place = operands
        context_key_rows = keys[keeper_row, position_row].reshape(-1, KEY_VALUE_HEADS * HEAD_WIDTH)
        context_value_rows = values[keeper_row, position_row].reshape(-1, KEY_VALUE_HEADS * HEAD_WIDTH)
        ctx_lengths = seg_lengths[keeper_row, position_row]
        allowed, query_live = allowed_mask(ctx_lengths, seg_lengths[leaf_index], inner_place, SEGMENT_SLOTS)
        local_query_rows = queries[leaf_index].reshape(2 * SEGMENT_SLOTS, QUERY_HEADS * HEAD_WIDTH)
        own_grad = out_grad[leaf_index].reshape(2 * SEGMENT_SLOTS, QUERY_HEADS * HEAD_WIDTH)
        query_gradient_block, key_gradient_block, value_gradient_block = attend_backward(local_query_rows, context_key_rows, context_value_rows, own_grad, allowed, query_live)
        return (query_gradient_block, key_gradient_block.reshape(BRANCH_DEPTH + 2, SEGMENT_SLOTS, KEY_VALUE_HEADS * HEAD_WIDTH), value_gradient_block.reshape(BRANCH_DEPTH + 2, SEGMENT_SLOTS, KEY_VALUE_HEADS * HEAD_WIDTH))
    query_gradient_block, key_gradient_block, value_gradient_block = lax.map(per_device, (jnp.arange(N_LEAF, dtype=jnp.int32), jnp.asarray(owners), jnp.asarray(slot_index), jnp.asarray(places)))
    keeper_lookup = jnp.asarray(owners)
    position_lookup = jnp.asarray(slot_index)
    key_grand_sum = jnp.zeros((N_LEAF, 2, SEGMENT_SLOTS, KEY_VALUE_HEADS * HEAD_WIDTH), jnp.float32).at[keeper_lookup, position_lookup].add(key_gradient_block)
    value_grand_sum = jnp.zeros((N_LEAF, 2, SEGMENT_SLOTS, KEY_VALUE_HEADS * HEAD_WIDTH), jnp.float32).at[keeper_lookup, position_lookup].add(value_gradient_block)
    grad_queries = query_gradient_block.reshape(N_LEAF, 2, SEGMENT_SLOTS, QUERY_HEADS * HEAD_WIDTH).astype(jnp.bfloat16)
    return (grad_queries, key_grand_sum.astype(jnp.bfloat16), value_grand_sum.astype(jnp.bfloat16))
```

```python
import functools
import math

import jax
import jax.numpy as jnp
from jax import lax
from jax.experimental import pallas as pl
from jax.experimental.pallas import tpu as pltpu
from jax.sharding import PartitionSpec as P

HEADS = 8
GROUP = 5
D = 128
R = 128
BIG = 2.0**30
SCALE = 1.0 / math.sqrt(D)
EXP2_SCALE = SCALE * math.log2(math.e)
CHUNKS = (4, 4)

SWAP = ((0, 1), (1, 0), (2, 3), (3, 2))
ONWARD = ((0, 3), (1, 2), (2, 1), (3, 0))
X_SWAP = [(4 * y + s, 4 * y + t) for y in range(4) for s, t in SWAP]
X_ONWARD = [(4 * y + s, 4 * y + t) for y in range(4) for s, t in ONWARD]
Y_SWAP = [(4 * s + x, 4 * t + x) for x in range(4) for s, t in SWAP]
Y_ONWARD = [(4 * s + x, 4 * t + x) for x in range(4) for s, t in ONWARD]


def dot(a, b, ca, cb):
    return lax.dot_general(a, b, (((ca,), (cb,)), ((), ())), preferred_element_type=jnp.float32)


def kernel(count, info, q_ref, g_ref, *refs):
    k_refs, v_refs = refs[0:6], refs[6:12]
    dq_ref, out_refs = refs[-11], refs[-10:-4]
    w_s, ds_s, mask_s, tri_s = refs[-4:]
    bf = jnp.bfloat16
    row = lax.broadcasted_iota(jnp.int32, (R, D), 0)
    col = lax.broadcasted_iota(jnp.int32, (R, D), 1)

    @pl.when(pl.program_id(0) == 0)
    def _():
        tri_s[...] = jnp.where((col == 0) | (col > row), -BIG, 0.0).astype(bf)
        for t in range(2):
            for j in range(6):
                hot = (col == 0) & (row >= info[6 * t + j])
                if (t, j) in ((0, 0), (1, 5)):
                    hot = hot | ((col == row) & (col > 0))
                mask_s[t, j * R : (j + 1) * R, :] = jnp.where(hot, 1.0, 0.0).astype(bf)

    k = jnp.concatenate([r[...] for r in k_refs], axis=0)
    v = jnp.concatenate([r[...] for r in v_refs], axis=0)
    qs, gs = [], []
    for t in range(2):
        live = row < info[12 + t]
        heads = [slice(h * D, (h + 1) * D) for h in range(GROUP)]
        rows = slice(t * R, (t + 1) * R)
        qs.append(jnp.concatenate([q_ref[rows, h] for h in heads], axis=0))
        gs.append(
            jnp.concatenate([jnp.where(live, g_ref[rows, h], jnp.zeros((), bf)) for h in heads], axis=0)
        )
    tri = jnp.concatenate([tri_s[...]] * GROUP, axis=0)
    for t, places in ((0, 5), (1, 6)):
        n = places * R
        k_wide = jnp.concatenate([k[:n], mask_s[t, :n, :]], axis=1)
        q_wide = jnp.concatenate([qs[t], tri], axis=1)
        k_turned = k[:n].T
        for h0, h1 in ((0, 2), (2, 4), (4, 5)):
            part = slice(h0 * R, h1 * R)
            place = slice((t * GROUP + h0) * R, (t * GROUP + h1) * R)
            s = dot(k_wide, q_wide[part], 1, 1)
            dw = dot(v[:n], gs[t][part], 1, 1)
            m = jnp.max(s, axis=0, keepdims=True)
            e = jnp.exp2((s - m) * EXP2_SCALE)
            w = e * (1.0 / jnp.sum(e, axis=0, keepdims=True))
            delta = jnp.sum(w * dw, axis=0, keepdims=True)
            ds = (w * (dw - delta)).astype(bf)
            w_s[:n, place] = w.astype(bf)
            ds_s[:n, place] = ds
            dq = (dot(k_turned, ds, 1, 0) * SCALE).T
            for h in range(h0, h1):
                dq_ref[t * R : (t + 1) * R, h * D : (h + 1) * D] = dq[
                    (h - h0) * R : (h - h0 + 1) * R
                ].astype(bf)
    q_all = jnp.concatenate(qs, axis=0)
    g_all = jnp.concatenate(gs, axis=0)
    n = 5 * R
    dk = dot(ds_s[:n, :], q_all, 1, 0) * SCALE
    dv = dot(w_s[:n, :], g_all, 1, 0)
    i = pl.program_id(0)
    k_cols = pl.ds(pl.multiple_of(i * D, D), D)
    v_cols = pl.ds(pl.multiple_of((count + i) * D, D), D)
    for j in range(5):
        out_refs[j][:, k_cols] = dk[j * R : (j + 1) * R].astype(out_refs[j].dtype)
        out_refs[j][:, v_cols] = dv[j * R : (j + 1) * R].astype(out_refs[j].dtype)
    out_refs[5][:, k_cols] = (dot(ds_s[n:, GROUP * R :], qs[1], 1, 0) * SCALE).astype(bf)
    out_refs[5][:, v_cols] = dot(w_s[n:, GROUP * R :], gs[1], 1, 0).astype(bf)


def attend_backward(info, q, g, k_slots, v_slots, first, count, grad_queries):
    specs = [pl.BlockSpec((2 * R, GROUP * D), lambda i, _: (0, first + i))] * 2
    arrays = [q, g]
    for array, block, offset in k_slots + v_slots:
        specs.append(pl.BlockSpec((R, D), functools.partial(lambda b, o, i, _: (b, o + i), block, offset)))
        arrays.append(array)
    kinds = [jnp.float32] + [jnp.bfloat16] * 5
    aliases = {}
    if grad_queries is not None:
        aliases = {1 + len(arrays): 0}
        specs.append(pl.BlockSpec(memory_space=pl.ANY))
        arrays.append(grad_queries)
    return pl.pallas_call(
        functools.partial(kernel, count),
        input_output_aliases=aliases,
        out_shape=[jax.ShapeDtypeStruct(q.shape, jnp.bfloat16)]
        + [jax.ShapeDtypeStruct((R, count * 2 * D), kind) for kind in kinds],
        grid_spec=pltpu.PrefetchScalarGridSpec(
            num_scalar_prefetch=1,
            grid=(count,),
            in_specs=specs,
            out_specs=[pl.BlockSpec((2 * R, GROUP * D), lambda i, _: (0, first + i))]
            + [pl.BlockSpec((R, count * 2 * D), lambda i, _: (0, 0))] * 6,
            scratch_shapes=[
                pltpu.VMEM((6 * R, 2 * GROUP * R), jnp.bfloat16),
                pltpu.VMEM((6 * R, 2 * GROUP * R), jnp.bfloat16),
                pltpu.VMEM((2, 6 * R, D), jnp.bfloat16),
                pltpu.VMEM((R, D), jnp.bfloat16),
            ],
        ),
        compiler_params=pltpu.CompilerParams(vmem_limit_bytes=40 * 2**20),
        cost_estimate=pl.CostEstimate(
            flops=count * 3_000_000_000, bytes_accessed=count * 2**20, transcendentals=count * 900_000
        ),
    )(info, *arrays)


def neighbours(x):
    swap = x ^ 1
    onward = jnp.where(x < 2, 2, 0)
    return swap, onward


def place_of(index):
    place = jnp.zeros_like(index)
    for bit in (3, 2, 1, 0):
        place = jnp.where((index >> bit) & 1 == 1, 4 - bit, place)
    return place


def shards(queries, keys, values, out_grad, seg_lengths):
    me = lax.axis_index("leaf")
    x, y = me & 3, me >> 2
    x_even, y_even = (x & 1) == 0, (y & 1) == 0
    x_swap, x_on = neighbours(x)
    y_swap, y_on = neighbours(y)
    ids = jnp.stack([me, 4 * y + x_swap, 4 * y + x_on, 4 * y_swap, 4 * y_on, me])
    lengths = jnp.take(seg_lengths[:, 0], ids).at[5].set(jnp.take(seg_lengths[:, 1], me))
    my_place = place_of(me)
    inner_limit = jnp.where((place_of(ids) < my_place) | (ids == me), lengths, 0)
    info = jnp.concatenate([inner_limit, lengths, lengths[:1], lengths[5:], jnp.zeros((2,), jnp.int32)])

    q = queries.reshape(2 * R, -1)
    g = out_grad.reshape(2 * R, -1)
    keys2, values2 = keys.reshape(2 * R, -1), values.reshape(2 * R, -1)

    def permute(array, pairs):
        return lax.ppermute(array, "leaf", pairs)

    grad_queries = None
    inner, leaf = [], []
    first = 0
    for count in CHUNKS:
        cols = slice(first * D, (first + count) * D)
        own = jnp.concatenate([keys2[:R, cols], values2[:R, cols]], axis=1)
        a = permute(own, X_SWAP)
        b = permute(jnp.where(x_even, own, a), X_ONWARD)
        upper = jnp.where(x == 0, own, jnp.where(x == 1, a, b))
        c = permute(upper, Y_SWAP)
        d = permute(jnp.where(y_even, upper, c), Y_ONWARD)
        got = [a, b, c, d]
        k_slots = [(keys2, 0, first)] + [(s, 0, 0) for s in got] + [(keys2, 1, first)]
        v_slots = [(values2, 0, first)] + [(s, 0, count) for s in got] + [(values2, 1, first)]
        grad_queries, g_own, g_a, g_b, g_c, g_d, g_leaf = attend_backward(
            info, q, g, k_slots, v_slots, first, count, grad_queries
        )
        f32, bf = jnp.float32, jnp.bfloat16
        back = permute(g_d, Y_ONWARD).astype(f32)
        up = jnp.where(y_even, back, 0.0)
        back2 = permute((g_c.astype(f32) + jnp.where(y_even, 0.0, back)).astype(bf), Y_SWAP).astype(f32)
        up = up + back2
        g_own = g_own + jnp.where(x == 0, up, 0.0)
        g_a = g_a.astype(f32) + jnp.where(x == 1, up, 0.0)
        g_b = g_b.astype(f32) + jnp.where(x >= 2, up, 0.0)
        back = permute(g_b.astype(bf), X_ONWARD).astype(f32)
        back2 = permute((g_a + jnp.where(x_even, 0.0, back)).astype(bf), X_SWAP).astype(f32)
        g_own = g_own + jnp.where(x_even, back, 0.0) + back2
        inner.append(g_own.astype(bf))
        leaf.append(g_leaf)
        first += count

    def assemble(half):
        rows = []
        for pieces in (inner, leaf):
            cut = [p[:, half * c * D : (half + 1) * c * D] for p, c in zip(pieces, CHUNKS)]
            rows.append(jnp.concatenate(cut, axis=1))
        return jnp.stack(rows)[None]

    return grad_queries.reshape(queries.shape), assemble(0), assemble(1)


def solution(mesh):
    rows = P(("prompt", "leaf"), None, None, None)
    return jax.shard_map(
        shards,
        mesh=mesh,
        in_specs=(rows, rows, rows, rows, P("prompt", None)),
        out_specs=(rows, rows, rows),
        check_vma=False,
    )
```

```python
import functools
import math

import jax
import jax.numpy as jnp
from jax import lax
from jax.experimental import pallas as pl
from jax.experimental.pallas import tpu as pltpu
from jax.sharding import PartitionSpec as P

HEADS = 8
GROUP = 5
D = 128
R = 128
BIG = 2.0**30
SCALE = 1.0 / math.sqrt(D)
EXP2_SCALE = SCALE * math.log2(math.e)
CHUNKS = (3, 3, 2)

SWAP = ((0, 1), (1, 0), (2, 3), (3, 2))
ONWARD = ((0, 3), (1, 2), (2, 1), (3, 0))
X_SWAP = [(4 * y + s, 4 * y + t) for y in range(4) for s, t in SWAP]
X_ONWARD = [(4 * y + s, 4 * y + t) for y in range(4) for s, t in ONWARD]
Y_SWAP = [(4 * s + x, 4 * t + x) for x in range(4) for s, t in SWAP]
Y_ONWARD = [(4 * s + x, 4 * t + x) for x in range(4) for s, t in ONWARD]


def dot(a, b, ca, cb):
    return lax.dot_general(a, b, (((ca,), (cb,)), ((), ())), preferred_element_type=jnp.float32)


def kernel(count, info, q_ref, g_ref, *refs):
    k_refs, v_refs = refs[0:6], refs[6:12]
    dq_ref, out_refs = refs[-11], refs[-10:-4]
    w_s, ds_s, mask_s, tri_s = refs[-4:]
    bf = jnp.bfloat16
    row = lax.broadcasted_iota(jnp.int32, (R, D), 0)
    col = lax.broadcasted_iota(jnp.int32, (R, D), 1)

    @pl.when(pl.program_id(0) == 0)
    def _():
        tri_s[...] = jnp.where((col == 0) | (col > row), -BIG, 0.0).astype(bf)
        for t in range(2):
            for j in range(6):
                hot = (col == 0) & (row >= info[6 * t + j])
                if (t, j) in ((0, 0), (1, 5)):
                    hot = hot | ((col == row) & (col > 0))
                mask_s[t, j * R : (j + 1) * R, :] = jnp.where(hot, 1.0, 0.0).astype(bf)

    k = jnp.concatenate([r[...] for r in k_refs], axis=0)
    v = jnp.concatenate([r[...] for r in v_refs], axis=0)
    qs, gs = [], []
    for t in range(2):
        live = row < info[12 + t]
        heads = [slice(h * D, (h + 1) * D) for h in range(GROUP)]
        rows = slice(t * R, (t + 1) * R)
        qs.append(jnp.concatenate([q_ref[rows, h] for h in heads], axis=0))
        gs.append(
            jnp.concatenate([jnp.where(live, g_ref[rows, h], jnp.zeros((), bf)) for h in heads], axis=0)
        )
    tri = jnp.concatenate([tri_s[...]] * GROUP, axis=0)
    sizes = (5 * R, 6 * R)
    k_wide = [jnp.concatenate([k[:n], mask_s[t, :n, :]], axis=1) for t, n in enumerate(sizes)]
    q_wide = [jnp.concatenate([qs[t], tri], axis=1) for t in range(2)]
    k_turned = k.T

    def products(t, h0, h1):
        n, part = sizes[t], slice(h0 * R, h1 * R)
        return dot(k_wide[t], q_wide[t][part], 1, 1), dot(v[:n], gs[t][part], 1, 1)

    def softmax_backward(t, h0, h1, s, dw):
        n, place = sizes[t], slice((t * GROUP + h0) * R, (t * GROUP + h1) * R)
        m = jnp.max(s, axis=0, keepdims=True)
        e = jnp.exp2((s - m) * EXP2_SCALE)
        w = e * (1.0 / jnp.sum(e, axis=0, keepdims=True))
        delta = jnp.sum(w * dw, axis=0, keepdims=True)
        w_s[:n, place] = w.astype(bf)
        ds_s[:n, place] = (w * (dw - delta)).astype(bf)

    total = {}

    def gradients(t, h0, h1):
        n, place = sizes[t], slice((t * GROUP + h0) * R, (t * GROUP + h1) * R)
        part = slice(h0 * R, h1 * R)
        ds = ds_s[:n, place]
        for name, term in (
            (("k", t), dot(ds, qs[t][part], 1, 0)),
            (("v", t), dot(w_s[:n, place], gs[t][part], 1, 0)),
        ):
            total[name] = term if name not in total else total[name] + term
        dq = (dot(k_turned[:, :n], ds, 1, 0) * SCALE).T
        for h in range(h0, h1):
            dq_ref[t * R : (t + 1) * R, h * D : (h + 1) * D] = dq[
                (h - h0) * R : (h - h0 + 1) * R
            ].astype(bf)

    todo = [(t, h0, h1) for t in range(2) for h0, h1 in ((0, 2), (2, 4), (4, 5))]
    ahead = products(*todo[0])
    for step, part in enumerate(todo):
        now = ahead
        if step + 1 < len(todo):
            ahead = products(*todo[step + 1])
        if step:
            gradients(*todo[step - 1])
        softmax_backward(*part, *now)
    gradients(*todo[-1])

    i = pl.program_id(0)
    n = 5 * R
    for name, at, scale in (("k", i, SCALE), ("v", count + i, 1.0)):
        cols = pl.ds(pl.multiple_of(at * D, D), D)
        inner, leaf = total[name, 0], total[name, 1]
        both = (inner + leaf[:n]) * scale
        for j in range(5):
            out_refs[j][:, cols] = both[j * R : (j + 1) * R].astype(out_refs[j].dtype)
        out_refs[5][:, cols] = (leaf[n:] * scale).astype(bf)


def attend_backward(info, q, g, k_slots, v_slots, first, count, grad_queries):
    specs = [pl.BlockSpec((2 * R, GROUP * D), lambda i, _: (0, first + i))] * 2
    arrays = [q, g]
    for array, block, offset in k_slots + v_slots:
        specs.append(pl.BlockSpec((R, D), functools.partial(lambda b, o, i, _: (b, o + i), block, offset)))
        arrays.append(array)
    kinds = [jnp.float32] + [jnp.bfloat16] * 5
    aliases = {}
    if grad_queries is not None:
        aliases = {1 + len(arrays): 0}
        specs.append(pl.BlockSpec(memory_space=pl.ANY))
        arrays.append(grad_queries)
    return pl.pallas_call(
        functools.partial(kernel, count),
        input_output_aliases=aliases,
        out_shape=[jax.ShapeDtypeStruct(q.shape, jnp.bfloat16)]
        + [jax.ShapeDtypeStruct((R, count * 2 * D), kind) for kind in kinds],
        grid_spec=pltpu.PrefetchScalarGridSpec(
            num_scalar_prefetch=1,
            grid=(count,),
            in_specs=specs,
            out_specs=[pl.BlockSpec((2 * R, GROUP * D), lambda i, _: (0, first + i))]
            + [pl.BlockSpec((R, count * 2 * D), lambda i, _: (0, 0))] * 6,
            scratch_shapes=[
                pltpu.VMEM((6 * R, 2 * GROUP * R), jnp.bfloat16),
                pltpu.VMEM((6 * R, 2 * GROUP * R), jnp.bfloat16),
                pltpu.VMEM((2, 6 * R, D), jnp.bfloat16),
                pltpu.VMEM((R, D), jnp.bfloat16),
            ],
        ),
        compiler_params=pltpu.CompilerParams(vmem_limit_bytes=50 * 2**20),
        cost_estimate=pl.CostEstimate(
            flops=count * 4_600_000_000, bytes_accessed=count * 2**20, transcendentals=count * 900_000
        ),
    )(info, *arrays)


def neighbours(x):
    swap = x ^ 1
    onward = jnp.where(x < 2, 2, 0)
    return swap, onward


def place_of(index):
    place = jnp.zeros_like(index)
    for bit in (3, 2, 1, 0):
        place = jnp.where((index >> bit) & 1 == 1, 4 - bit, place)
    return place


def shards(queries, keys, values, out_grad, seg_lengths):
    me = lax.axis_index("leaf")
    x, y = me & 3, me >> 2
    x_even, y_even = (x & 1) == 0, (y & 1) == 0
    x_swap, x_on = neighbours(x)
    y_swap, y_on = neighbours(y)
    ids = jnp.stack([me, 4 * y + x_swap, 4 * y + x_on, 4 * y_swap, 4 * y_on, me])
    lengths = jnp.take(seg_lengths[:, 0], ids).at[5].set(jnp.take(seg_lengths[:, 1], me))
    my_place = place_of(me)
    inner_limit = jnp.where((place_of(ids) < my_place) | (ids == me), lengths, 0)
    info = jnp.concatenate([inner_limit, lengths, lengths[:1], lengths[5:], jnp.zeros((2,), jnp.int32)])

    q = queries.reshape(2 * R, -1)
    g = out_grad.reshape(2 * R, -1)
    keys2, values2 = keys.reshape(2 * R, -1), values.reshape(2 * R, -1)

    def permute(array, pairs):
        return lax.ppermute(array, "leaf", pairs)

    grad_queries = None
    inner, leaf = [], []
    first = 0
    for count in CHUNKS:
        cols = slice(first * D, (first + count) * D)
        own = jnp.concatenate([keys2[:R, cols], values2[:R, cols]], axis=1)
        if first:
            own, _ = lax.optimization_barrier((own, a))
        a = permute(own, X_SWAP)
        b = permute(jnp.where(x_even, own, a), X_ONWARD)
        upper = jnp.where(x == 0, own, jnp.where(x == 1, a, b))
        c = permute(upper, Y_SWAP)
        d = permute(jnp.where(y_even, upper, c), Y_ONWARD)
        got = [a, b, c, d]
        k_slots = [(keys2, 0, first)] + [(s, 0, 0) for s in got] + [(keys2, 1, first)]
        v_slots = [(values2, 0, first)] + [(s, 0, count) for s in got] + [(values2, 1, first)]
        grad_queries, g_own, g_a, g_b, g_c, g_d, g_leaf = attend_backward(
            info, q, g, k_slots, v_slots, first, count, grad_queries
        )
        f32, bf = jnp.float32, jnp.bfloat16
        back = permute(g_d, Y_ONWARD).astype(f32)
        up = jnp.where(y_even, back, 0.0)
        back2 = permute((g_c.astype(f32) + jnp.where(y_even, 0.0, back)).astype(bf), Y_SWAP).astype(f32)
        up = up + back2
        g_own = g_own + jnp.where(x == 0, up, 0.0)
        g_a = g_a.astype(f32) + jnp.where(x == 1, up, 0.0)
        g_b = g_b.astype(f32) + jnp.where(x >= 2, up, 0.0)
        back = permute(g_b.astype(bf), X_ONWARD).astype(f32)
        back2 = permute((g_a + jnp.where(x_even, 0.0, back)).astype(bf), X_SWAP).astype(f32)
        g_own = g_own + jnp.where(x_even, back, 0.0) + back2
        inner.append(g_own.astype(bf))
        leaf.append(g_leaf)
        first += count

    def assemble(half):
        rows = []
        for pieces in (inner, leaf):
            cut = [p[:, half * c * D : (half + 1) * c * D] for p, c in zip(pieces, CHUNKS)]
            rows.append(jnp.concatenate(cut, axis=1))
        return jnp.stack(rows)[None]

    return grad_queries.reshape(queries.shape), assemble(0), assemble(1)


def solution(mesh):
    rows = P(("prompt", "leaf"), None, None, None)
    return jax.shard_map(
        shards,
        mesh=mesh,
        in_specs=(rows, rows, rows, rows, P("prompt", None)),
        out_specs=(rows, rows, rows),
        check_vma=False,
    )
```

```python
import functools
import math

import jax
import jax.numpy as jnp
from jax import lax
from jax.experimental import pallas as pl
from jax.experimental.pallas import tpu as pltpu
from jax.sharding import PartitionSpec as P

HEADS = 8
GROUP = 5
D = 128
R = 128
BIG = 2.0**30
SCALE = 1.0 / math.sqrt(D)
EXP2_SCALE = SCALE * math.log2(math.e)
CHUNKS = (3, 3, 2)

SWAP = ((0, 1), (1, 0), (2, 3), (3, 2))
ONWARD = ((0, 3), (1, 2), (2, 1), (3, 0))
X_SWAP = [(4 * y + s, 4 * y + t) for y in range(4) for s, t in SWAP]
X_ONWARD = [(4 * y + s, 4 * y + t) for y in range(4) for s, t in ONWARD]
Y_SWAP = [(4 * s + x, 4 * t + x) for x in range(4) for s, t in SWAP]
Y_ONWARD = [(4 * s + x, 4 * t + x) for x in range(4) for s, t in ONWARD]


def dot(a, b, ca, cb):
    return lax.dot_general(a, b, (((ca,), (cb,)), ((), ())), preferred_element_type=jnp.float32)


def stacked(q_ref, g_ref, info):
    row = lax.broadcasted_iota(jnp.int32, (R, D), 0)
    qs, gs = [], []
    for t in range(2):
        live = row < info[12 + t]
        heads = [slice(h * D, (h + 1) * D) for h in range(GROUP)]
        rows = slice(t * R, (t + 1) * R)
        qs.append(jnp.concatenate([q_ref[rows, h] for h in heads], axis=0))
        gs.append(
            jnp.concatenate(
                [jnp.where(live, g_ref[rows, h], jnp.zeros((), jnp.bfloat16)) for h in heads], axis=0
            )
        )
    return qs, gs


def columns(count):
    i = pl.program_id(0)
    return [pl.ds(pl.multiple_of(at * D, D), D) for at in (i, count + i)]


def score_kernel(count, info, q_ref, g_ref, *refs):
    k_refs, v_refs = refs[0:6], refs[6:12]
    out_refs, ds_ref, wo_ref = refs[12:16], refs[16], refs[17]
    w_s, mask_s, tri_s = refs[18:21]
    bf = jnp.bfloat16
    row = lax.broadcasted_iota(jnp.int32, (R, D), 0)
    col = lax.broadcasted_iota(jnp.int32, (R, D), 1)

    @pl.when(pl.program_id(0) == 0)
    def _():
        tri_s[...] = jnp.where((col == 0) | (col > row), -BIG, 0.0).astype(bf)
        for t in range(2):
            for j in range(6):
                hot = (col == 0) & (row >= info[6 * t + j])
                if (t, j) in ((0, 0), (1, 5)):
                    hot = hot | ((col == row) & (col > 0))
                mask_s[t, j * R : (j + 1) * R, :] = jnp.where(hot, 1.0, 0.0).astype(bf)

    k = jnp.concatenate([r[...] for r in k_refs], axis=0)
    v = jnp.concatenate([r[...] for r in v_refs], axis=0)
    qs, gs = stacked(q_ref, g_ref, info)
    tri = jnp.concatenate([tri_s[...]] * GROUP, axis=0)
    sizes = (5 * R, 6 * R)
    k_wide = [jnp.concatenate([k[:n], mask_s[t, :n, :]], axis=1) for t, n in enumerate(sizes)]
    q_wide = [jnp.concatenate([qs[t], tri], axis=1) for t in range(2)]

    def products(t, h0, h1):
        n, part = sizes[t], slice(h0 * R, h1 * R)
        return dot(k_wide[t], q_wide[t][part], 1, 1), dot(v[:n], gs[t][part], 1, 1)

    def softmax_backward(t, h0, h1, s, dw):
        n, place = sizes[t], slice((t * GROUP + h0) * R, (t * GROUP + h1) * R)
        m = jnp.max(s, axis=0, keepdims=True)
        e = jnp.exp2((s - m) * EXP2_SCALE)
        w = e * (1.0 / jnp.sum(e, axis=0, keepdims=True))
        delta = jnp.sum(w * dw, axis=0, keepdims=True)
        ds_ref[:n, place] = (w * (dw - delta)).astype(bf)
        w_half = w.astype(bf)
        wo_ref[:R, place] = w_half[:R]
        w_s[:, place] = w_half[R : 5 * R]
        if t:
            wo_ref[R:, place] = w_half[5 * R :]

    total = []

    def gradients(t, h0, h1):
        place, part = slice((t * GROUP + h0) * R, (t * GROUP + h1) * R), slice(h0 * R, h1 * R)
        terms = [
            dot(ds_ref[R : 5 * R, place], qs[t][part], 1, 0),
            dot(w_s[:, place], gs[t][part], 1, 0),
        ]
        total[:] = [a + b for a, b in zip(total, terms)] if total else terms

    todo = [(t, h0, h1) for t in range(2) for h0, h1 in ((0, 2), (2, 4), (4, 5))]
    ahead = products(*todo[0])
    for step, part in enumerate(todo):
        now = ahead
        if step + 1 < len(todo):
            ahead = products(*todo[step + 1])
        if step:
            gradients(*todo[step - 1])
        softmax_backward(*part, *now)
    gradients(*todo[-1])
    for cols, value, scale in zip(columns(count), total, (SCALE, 1.0)):
        for j in range(4):
            out_refs[j][:, cols] = (value[j * R : (j + 1) * R] * scale).astype(bf)


def own_kernel(count, info, q_ref, g_ref, *refs):
    k_refs, ds_ref, wo_ref = refs[0:6], refs[6], refs[7]
    dq_ref, inner_ref, leaf_ref = refs[-3:]
    bf = jnp.bfloat16
    k_turned = jnp.concatenate([r[...] for r in k_refs], axis=0).T
    qs, gs = stacked(q_ref, g_ref, info)
    half = GROUP * R
    for t, n in ((0, 5 * R), (1, 6 * R)):
        dq = (dot(k_turned[:, :n], ds_ref[:n, t * half : (t + 1) * half], 1, 0) * SCALE).T
        for h in range(GROUP):
            dq_ref[t * R : (t + 1) * R, h * D : (h + 1) * D] = dq[h * R : (h + 1) * R].astype(bf)
    k_cols, v_cols = columns(count)
    inner_ref[:, k_cols] = dot(ds_ref[:R, :], jnp.concatenate(qs, axis=0), 1, 0) * SCALE
    inner_ref[:, v_cols] = dot(wo_ref[:R, :], jnp.concatenate(gs, axis=0), 1, 0)
    leaf_ref[:, k_cols] = (dot(ds_ref[5 * R :, half:], qs[1], 1, 0) * SCALE).astype(bf)
    leaf_ref[:, v_cols] = dot(wo_ref[R:, half:], gs[1], 1, 0).astype(bf)


def slot_specs(slots):
    return [
        pl.BlockSpec((R, D), functools.partial(lambda b, o, i, _: (b, o + i), block, offset))
        for _, block, offset in slots
    ]


def score_gradients(info, q, g, k_slots, v_slots, first, count):
    bf = jnp.bfloat16
    wide = 2 * GROUP * R
    return pl.pallas_call(
        functools.partial(score_kernel, count),
        out_shape=[jax.ShapeDtypeStruct((R, count * 2 * D), bf)] * 4
        + [jax.ShapeDtypeStruct((count * n * R, wide), bf) for n in (6, 2)],
        grid_spec=pltpu.PrefetchScalarGridSpec(
            num_scalar_prefetch=1,
            grid=(count,),
            in_specs=[pl.BlockSpec((2 * R, GROUP * D), lambda i, _: (0, first + i))] * 2
            + slot_specs(k_slots + v_slots),
            out_specs=[pl.BlockSpec((R, count * 2 * D), lambda i, _: (0, 0))] * 4
            + [pl.BlockSpec((n * R, wide), lambda i, _: (i, 0)) for n in (6, 2)],
            scratch_shapes=[
                pltpu.VMEM((4 * R, wide), bf),
                pltpu.VMEM((2, 6 * R, D), bf),
                pltpu.VMEM((R, D), bf),
            ],
        ),
        compiler_params=pltpu.CompilerParams(vmem_limit_bytes=50 * 2**20),
        cost_estimate=pl.CostEstimate(
            flops=count * 3_600_000_000, bytes_accessed=count * 2**22, transcendentals=count * 900_000
        ),
    )(info, q, g, *[s[0] for s in k_slots + v_slots])


def own_gradients(info, q, g, k_slots, ds, wo, first, count, grad_queries):
    wide = 2 * GROUP * R
    specs = [pl.BlockSpec((2 * R, GROUP * D), lambda i, _: (0, first + i))] * 2 + slot_specs(k_slots)
    specs += [pl.BlockSpec((n * R, wide), lambda i, _: (i, 0)) for n in (6, 2)]
    arrays = [q, g] + [s[0] for s in k_slots] + [ds, wo]
    aliases = {}
    if grad_queries is not None:
        aliases = {1 + len(arrays): 0}
        specs.append(pl.BlockSpec(memory_space=pl.ANY))
        arrays.append(grad_queries)
    return pl.pallas_call(
        functools.partial(own_kernel, count),
        input_output_aliases=aliases,
        out_shape=[
            jax.ShapeDtypeStruct(q.shape, jnp.bfloat16),
            jax.ShapeDtypeStruct((R, count * 2 * D), jnp.float32),
            jax.ShapeDtypeStruct((R, count * 2 * D), jnp.bfloat16),
        ],
        grid_spec=pltpu.PrefetchScalarGridSpec(
            num_scalar_prefetch=1,
            grid=(count,),
            in_specs=specs,
            out_specs=[pl.BlockSpec((2 * R, GROUP * D), lambda i, _: (0, first + i))]
            + [pl.BlockSpec((R, count * 2 * D), lambda i, _: (0, 0))] * 2,
        ),
        compiler_params=pltpu.CompilerParams(vmem_limit_bytes=50 * 2**20),
        cost_estimate=pl.CostEstimate(
            flops=count * 1_300_000_000, bytes_accessed=count * 2**22, transcendentals=0
        ),
    )(info, *arrays)


def neighbours(x):
    swap = x ^ 1
    onward = jnp.where(x < 2, 2, 0)
    return swap, onward


def place_of(index):
    place = jnp.zeros_like(index)
    for bit in (3, 2, 1, 0):
        place = jnp.where((index >> bit) & 1 == 1, 4 - bit, place)
    return place


def shards(queries, keys, values, out_grad, seg_lengths):
    me = lax.axis_index("leaf")
    x, y = me & 3, me >> 2
    x_even, y_even = (x & 1) == 0, (y & 1) == 0
    x_swap, x_on = neighbours(x)
    y_swap, y_on = neighbours(y)
    ids = jnp.stack([me, 4 * y + x_swap, 4 * y + x_on, 4 * y_swap, 4 * y_on, me])
    lengths = jnp.take(seg_lengths[:, 0], ids).at[5].set(jnp.take(seg_lengths[:, 1], me))
    my_place = place_of(me)
    inner_limit = jnp.where((place_of(ids) < my_place) | (ids == me), lengths, 0)
    info = jnp.concatenate([inner_limit, lengths, lengths[:1], lengths[5:], jnp.zeros((2,), jnp.int32)])

    q = queries.reshape(2 * R, -1)
    g = out_grad.reshape(2 * R, -1)
    keys2, values2 = keys.reshape(2 * R, -1), values.reshape(2 * R, -1)

    f32, bf = jnp.float32, jnp.bfloat16
    firsts = [sum(CHUNKS[:c]) for c in range(len(CHUNKS))]
    sent, got, scored, owned = {}, {}, {}, {}

    def hop(number, c):
        pairs = (X_SWAP, X_ONWARD, Y_SWAP, Y_ONWARD, Y_ONWARD, Y_SWAP, X_ONWARD, X_SWAP)[number]
        if number == 0:
            cols = slice(firsts[c] * D, (firsts[c] + CHUNKS[c]) * D)
            value = sent[c] = jnp.concatenate([keys2[:R, cols], values2[:R, cols]], axis=1)
        elif number == 1:
            value = jnp.where(x_even, sent[c], got[0, c])
        elif number == 2:
            value = sent[c] = jnp.where(x == 0, sent[c], jnp.where(x == 1, got[0, c], got[1, c]))
        elif number == 3:
            value = jnp.where(y_even, sent[c], got[2, c])
        elif number == 4:
            value = scored[c][3]
        elif number == 5:
            value = (scored[c][2].astype(f32) + jnp.where(y_even, 0.0, got[4, c].astype(f32))).astype(bf)
        else:
            upper = jnp.where(y_even, got[4, c].astype(f32), 0.0) + got[5, c].astype(f32)
            if number == 6:
                value = (scored[c][1].astype(f32) + jnp.where(x >= 2, upper, 0.0)).astype(bf)
            else:
                value = scored[c][0].astype(f32) + jnp.where(x == 1, upper, 0.0)
                value = (value + jnp.where(x_even, 0.0, got[6, c].astype(f32))).astype(bf)
        return value, pairs

    def stage(hops, after):
        values, pairs = zip(*[hop(*h) for h in hops])
        if after:
            values = lax.optimization_barrier((values, tuple(after)))[0]
        for h, value, p in zip(hops, values, pairs):
            got[h] = lax.ppermute(value, "leaf", p)
        return [got[h] for h in hops]

    def slots(c):
        keys_in = [(keys2, 0, firsts[c])] + [(got[n, c], 0, 0) for n in range(4)] + [(keys2, 1, firsts[c])]
        values_in = [(values2, 0, firsts[c])] + [(got[n, c], 0, CHUNKS[c]) for n in range(4)]
        return keys_in, values_in + [(values2, 1, firsts[c])]

    def score(c, after):
        held = lax.optimization_barrier((info, tuple(after)))[0]
        scored[c] = score_gradients(held, q, g, *slots(c), firsts[c], CHUNKS[c])
        return list(scored[c][:1])

    grad_queries = None

    def own(c, after):
        held = lax.optimization_barrier((info, tuple(after)))[0]
        ds, wo = scored[c][4:]
        owned[c] = own_gradients(held, q, g, slots(c)[0], ds, wo, firsts[c], CHUNKS[c], grad_queries)
        return owned[c][0], list(owned[c][1:2])

    last = stage([(0, 0)], [])
    last = stage([(1, 0), (0, 1)], last)
    last = stage([(2, 0), (1, 1), (0, 2)], last)
    last = stage([(3, 0), (2, 1), (1, 2)], last)
    ready, last = last, stage([(3, 1), (2, 2)], last)
    done = score(0, ready)
    ready, last = last, stage([(3, 2), (4, 0)], last + done)
    done = score(1, ready + done)
    ready, last = last, stage([(5, 0), (4, 1)], last + done)
    done = score(2, ready + done)
    ready, last = last, stage([(4, 2), (5, 1), (6, 0)], last + done)
    grad_queries, done = own(0, ready + done)
    ready, last = last, stage([(5, 2), (6, 1), (7, 0)], last + done)
    grad_queries, done = own(1, ready + done)
    ready, last = last, stage([(6, 2), (7, 1)], last + done)
    grad_queries, done = own(2, ready + done)
    stage([(7, 2)], last + done)

    inner, leaf = [], []
    for c in range(len(CHUNKS)):
        upper = jnp.where(y_even, got[4, c].astype(f32), 0.0) + got[5, c].astype(f32)
        mine = owned[c][1] + jnp.where(x == 0, upper, 0.0)
        mine = mine + jnp.where(x_even, got[6, c].astype(f32), 0.0) + got[7, c].astype(f32)
        inner.append(mine.astype(bf))
        leaf.append(owned[c][2])

    def assemble(half):
        rows = []
        for pieces in (inner, leaf):
            cut = [p[:, half * c * D : (half + 1) * c * D] for p, c in zip(pieces, CHUNKS)]
            rows.append(jnp.concatenate(cut, axis=1))
        return jnp.stack(rows)[None]

    return grad_queries.reshape(queries.shape), assemble(0), assemble(1)


def solution(mesh):
    rows = P(("prompt", "leaf"), None, None, None)
    return jax.shard_map(
        shards,
        mesh=mesh,
        in_specs=(rows, rows, rows, rows, P("prompt", None)),
        out_specs=(rows, rows, rows),
        check_vma=False,
    )
```

```python
import functools
import math

import jax
import jax.numpy as jnp
from jax import lax
from jax.experimental import pallas as pl
from jax.experimental.pallas import tpu as pltpu
from jax.sharding import PartitionSpec as P

HEADS = 8
GROUP = 5
D = 128
R = 128
BIG = 2.0**30
SCALE = 1.0 / math.sqrt(D)
EXP2_SCALE = SCALE * math.log2(math.e)
CHUNKS = (4, 4)

SWAP = ((0, 1), (1, 0), (2, 3), (3, 2))
ONWARD = ((0, 3), (1, 2), (2, 1), (3, 0))


def pairs(axis, ring):
    if axis == "x":
        return [(4 * y + s, 4 * y + t) for y in range(4) for s, t in ring]
    return [(4 * s + x, 4 * t + x) for x in range(4) for s, t in ring]


def dot(a, b, ca, cb):
    return lax.dot_general(a, b, (((ca,), (cb,)), ((), ())), preferred_element_type=jnp.float32)


def kernel(count, info, q_ref, g_ref, *refs):
    k_refs, v_refs = refs[0:6], refs[6:12]
    dq_ref, out_refs = refs[-11], refs[-10:-4]
    w_s, ds_s, mask_s, tri_s = refs[-4:]
    bf = jnp.bfloat16
    row = lax.broadcasted_iota(jnp.int32, (R, D), 0)
    col = lax.broadcasted_iota(jnp.int32, (R, D), 1)

    @pl.when(pl.program_id(0) == 0)
    def _():
        tri_s[...] = jnp.where((col == 0) | (col > row), -BIG, 0.0).astype(bf)
        for t in range(2):
            for j in range(6):
                hot = (col == 0) & (row >= info[6 * t + j])
                if (t, j) in ((0, 0), (1, 5)):
                    hot = hot | ((col == row) & (col > 0))
                mask_s[t, j * R : (j + 1) * R, :] = jnp.where(hot, 1.0, 0.0).astype(bf)

    k = jnp.concatenate([r[...] for r in k_refs], axis=0)
    v = jnp.concatenate([r[...] for r in v_refs], axis=0)
    qs, gs = [], []
    for t in range(2):
        live = row < info[12 + t]
        heads = [slice(h * D, (h + 1) * D) for h in range(GROUP)]
        rows = slice(t * R, (t + 1) * R)
        qs.append(jnp.concatenate([q_ref[rows, h] for h in heads], axis=0))
        gs.append(
            jnp.concatenate([jnp.where(live, g_ref[rows, h], jnp.zeros((), bf)) for h in heads], axis=0)
        )
    tri = jnp.concatenate([tri_s[...]] * GROUP, axis=0)
    sizes = (5 * R, 6 * R)
    k_wide = [jnp.concatenate([k[:n], mask_s[t, :n, :]], axis=1) for t, n in enumerate(sizes)]
    q_wide = [jnp.concatenate([qs[t], tri], axis=1) for t in range(2)]
    k_turned = k.T

    def products(t, h0, h1):
        n, part = sizes[t], slice(h0 * R, h1 * R)
        return dot(k_wide[t], q_wide[t][part], 1, 1), dot(v[:n], gs[t][part], 1, 1)

    def softmax_backward(t, h0, h1, s, dw):
        n, place = sizes[t], slice((t * GROUP + h0) * R, (t * GROUP + h1) * R)
        m = jnp.max(s, axis=0, keepdims=True)
        e = jnp.exp2((s - m) * EXP2_SCALE)
        w = e * (1.0 / jnp.sum(e, axis=0, keepdims=True))
        delta = jnp.sum(w * dw, axis=0, keepdims=True)
        w_s[:n, place] = w.astype(bf)
        ds_s[:n, place] = (w * (dw - delta)).astype(bf)

    total = {}

    def gradients(t, h0, h1):
        n, place = sizes[t], slice((t * GROUP + h0) * R, (t * GROUP + h1) * R)
        part = slice(h0 * R, h1 * R)
        ds = ds_s[:n, place]
        for name, term in (
            (("k", t), dot(ds, qs[t][part], 1, 0)),
            (("v", t), dot(w_s[:n, place], gs[t][part], 1, 0)),
        ):
            total[name] = term if name not in total else total[name] + term
        dq = (dot(k_turned[:, :n], ds, 1, 0) * SCALE).T
        for h in range(h0, h1):
            dq_ref[t * R : (t + 1) * R, h * D : (h + 1) * D] = dq[
                (h - h0) * R : (h - h0 + 1) * R
            ].astype(bf)

    todo = [(t, h0, h1) for t in range(2) for h0, h1 in ((0, 2), (2, 4), (4, 5))]
    ahead = products(*todo[0])
    for step, part in enumerate(todo):
        now = ahead
        if step + 1 < len(todo):
            ahead = products(*todo[step + 1])
        if step:
            gradients(*todo[step - 1])
        softmax_backward(*part, *now)
    gradients(*todo[-1])

    i = pl.program_id(0)
    n = 5 * R
    for name, at, scale in (("k", i, SCALE), ("v", count + i, 1.0)):
        cols = pl.ds(pl.multiple_of(at * D, D), D)
        inner, leaf = total[name, 0], total[name, 1]
        both = (inner + leaf[:n]) * scale
        for j in range(5):
            out_refs[j][:, cols] = both[j * R : (j + 1) * R].astype(out_refs[j].dtype)
        out_refs[5][:, cols] = (leaf[n:] * scale).astype(bf)


def attend_backward(info, q, g, k_slots, v_slots, first, count, grad_queries):
    specs = [pl.BlockSpec((2 * R, GROUP * D), lambda i, _: (0, first + i))] * 2
    arrays = [q, g]
    for array, block, offset in k_slots + v_slots:
        specs.append(pl.BlockSpec((R, D), functools.partial(lambda b, o, i, _: (b, o + i), block, offset)))
        arrays.append(array)
    kinds = [jnp.float32] + [jnp.bfloat16] * 5
    aliases = {}
    if grad_queries is not None:
        aliases = {1 + len(arrays): 0}
        specs.append(pl.BlockSpec(memory_space=pl.ANY))
        arrays.append(grad_queries)
    return pl.pallas_call(
        functools.partial(kernel, count),
        input_output_aliases=aliases,
        out_shape=[jax.ShapeDtypeStruct(q.shape, jnp.bfloat16)]
        + [jax.ShapeDtypeStruct((R, count * 2 * D), kind) for kind in kinds],
        grid_spec=pltpu.PrefetchScalarGridSpec(
            num_scalar_prefetch=1,
            grid=(count,),
            in_specs=specs,
            out_specs=[pl.BlockSpec((2 * R, GROUP * D), lambda i, _: (0, first + i))]
            + [pl.BlockSpec((R, count * 2 * D), lambda i, _: (0, 0))] * 6,
            scratch_shapes=[
                pltpu.VMEM((6 * R, 2 * GROUP * R), jnp.bfloat16),
                pltpu.VMEM((6 * R, 2 * GROUP * R), jnp.bfloat16),
                pltpu.VMEM((2, 6 * R, D), jnp.bfloat16),
                pltpu.VMEM((R, D), jnp.bfloat16),
            ],
        ),
        compiler_params=pltpu.CompilerParams(vmem_limit_bytes=50 * 2**20),
        cost_estimate=pl.CostEstimate(
            flops=count * 4_600_000_000, bytes_accessed=count * 2**20, transcendentals=count * 900_000
        ),
    )(info, *arrays)


def neighbours(x):
    swap = x ^ 1
    onward = jnp.where(x < 2, 2, 0)
    return swap, onward


def place_of(index):
    place = jnp.zeros_like(index)
    for bit in (3, 2, 1, 0):
        place = jnp.where((index >> bit) & 1 == 1, 4 - bit, place)
    return place


def shards(queries, keys, values, out_grad, seg_lengths):
    me = lax.axis_index("leaf")
    x, y = me & 3, me >> 2
    x_even, y_even = (x & 1) == 0, (y & 1) == 0
    x_swap, x_on = neighbours(x)
    y_swap, y_on = neighbours(y)
    ids = jnp.stack([me, 4 * y + x_swap, 4 * y + x_on, 4 * y_swap, 4 * y_on, me])
    lengths = jnp.take(seg_lengths[:, 0], ids).at[5].set(jnp.take(seg_lengths[:, 1], me))
    my_place = place_of(me)
    inner_limit = jnp.where((place_of(ids) < my_place) | (ids == me), lengths, 0)
    info = jnp.concatenate([inner_limit, lengths, lengths[:1], lengths[5:], jnp.zeros((2,), jnp.int32)])

    q = queries.reshape(2 * R, -1)
    g = out_grad.reshape(2 * R, -1)
    keys2, values2 = keys.reshape(2 * R, -1), values.reshape(2 * R, -1)

    f32, bf = jnp.float32, jnp.bfloat16
    firsts = [sum(CHUNKS[:c]) for c in range(len(CHUNKS))]
    sent, got, scored = {}, {}, {}

    def permute(value, axis, ring):
        return lax.ppermute(value, "leaf", pairs(axis, ring))

    def tie(value, after):
        return lax.optimization_barrier((value, tuple(after)))[0] if after else value

    def upper_of(c):
        return jnp.where(x == 0, sent[c], jnp.where(x == 1, got["a", c], got["b", c]))

    def move(name, c, after):
        if name == "g0":
            cols = slice(firsts[c] * D, (firsts[c] + CHUNKS[c]) * D)
            sent[c] = tie(jnp.concatenate([keys2[:R, cols], values2[:R, cols]], axis=1), after)
            got["a", c] = permute(sent[c], "x", SWAP)
            return [got["a", c]]
        if name == "g1":
            got["b", c] = permute(tie(jnp.where(x_even, sent[c], got["a", c]), after), "x", ONWARD)
            return [got["b", c]]
        if name == "g2":
            got["u", c] = tie(upper_of(c), after)
            got["c", c] = permute(got["u", c], "y", SWAP)
            return [got["c", c]]
        if name == "g3":
            got["d", c] = permute(tie(jnp.where(y_even, got["u", c], got["c", c]), after), "y", ONWARD)
            return [got["d", c]]
        own, a, b, near, far = scored[c][1:6]
        up = got.get(("up", c))
        if name == "r0":
            got[name, c] = permute(tie(far, after), "y", ONWARD).astype(f32)
        elif name == "r1":
            value = near.astype(f32) + jnp.where(y_even, 0.0, got["r0", c])
            got[name, c] = permute(tie(value.astype(bf), after), "y", SWAP).astype(f32)
            got["up", c] = jnp.where(y_even, got["r0", c], 0.0) + got[name, c]
        elif name == "r2":
            value = b.astype(f32) + jnp.where(x >= 2, up, 0.0)
            got[name, c] = permute(tie(value.astype(bf), after), "x", ONWARD).astype(f32)
        else:
            value = a.astype(f32) + jnp.where(x == 1, up, 0.0) + jnp.where(x_even, 0.0, got["r2", c])
            got[name, c] = permute(tie(value.astype(bf), after), "x", SWAP).astype(f32)
            total = own + jnp.where(x == 0, up, 0.0) + jnp.where(x_even, got["r2", c], 0.0)
            got["own", c] = (total + got[name, c]).astype(bf)
        back = [got[name, c]]
        return back

    def stage(moves, after):
        return [r for name, c in moves for r in move(name, c, after)]

    def score(c, after):
        k_slots = [(keys2, 0, firsts[c])] + [(got[n, c], 0, 0) for n in "abcd"] + [(keys2, 1, firsts[c])]
        v_slots = [(values2, 0, firsts[c])] + [(got[n, c], 0, CHUNKS[c]) for n in "abcd"]
        v_slots += [(values2, 1, firsts[c])]
        before = scored[c - 1][0] if c else None
        scored[c] = attend_backward(tie(info, after), q, g, k_slots, v_slots, firsts[c], CHUNKS[c], before)
        return list(scored[c][1:2])

    s1 = stage([("g0", 0)], [])
    s2 = stage([("g1", 0)], []) + stage([("g0", 1)], s1)
    s3 = stage([("g2", 0), ("g1", 1)], [])
    s4 = stage([("g3", 0), ("g2", 1)], [])
    k0 = score(0, s4)
    s5 = stage([("g3", 1)], [])
    s6 = stage([("r0", 0)], s5 + k0)
    k1 = score(1, s5 + k0)
    s7 = stage([("r0", 1), ("r1", 0)], s6 + k1)
    s8 = stage([("r1", 1), ("r2", 0)], [])
    s9 = stage([("r2", 1), ("r3", 0)], [])
    stage([("r3", 1)], [])

    grad_queries = scored[len(CHUNKS) - 1][0]
    inner = [got["own", c] for c in range(len(CHUNKS))]
    leaf = [scored[c][6] for c in range(len(CHUNKS))]

    def assemble(half):
        rows = []
        for pieces in (inner, leaf):
            cut = [p[:, half * c * D : (half + 1) * c * D] for p, c in zip(pieces, CHUNKS)]
            rows.append(jnp.concatenate(cut, axis=1))
        return jnp.stack(rows)[None]

    return grad_queries.reshape(queries.shape), assemble(0), assemble(1)


def solution(mesh):
    rows = P(("prompt", "leaf"), None, None, None)
    return jax.shard_map(
        shards,
        mesh=mesh,
        in_specs=(rows, rows, rows, rows, P("prompt", None)),
        out_specs=(rows, rows, rows),
        check_vma=False,
    )
```

```python
import functools
import math

import jax
import jax.numpy as jnp
from jax import lax
from jax.experimental import pallas as pl
from jax.experimental.pallas import tpu as pltpu
from jax.sharding import PartitionSpec as P

HEADS = 8
GROUP = 5
D = 128
R = 128
BIG = 2.0**30
SCALE = 1.0 / math.sqrt(D)
EXP2_SCALE = SCALE * math.log2(math.e)
CHUNKS = (4, 4)

SWAP = ((0, 1), (1, 0), (2, 3), (3, 2))
ONWARD = ((0, 3), (1, 2), (2, 1), (3, 0))


def pairs(axis, ring):
    if axis == "x":
        return [(4 * y + s, 4 * y + t) for y in range(4) for s, t in ring]
    return [(4 * s + x, 4 * t + x) for x in range(4) for s, t in ring]


def dot(a, b, ca, cb):
    return lax.dot_general(a, b, (((ca,), (cb,)), ((), ())), preferred_element_type=jnp.float32)


def kernel(count, info, q_ref, g_ref, *refs):
    k_refs, v_refs = refs[0:6], refs[6:12]
    dq_ref, out_refs = refs[-12], refs[-11:-5]
    w_s, ds_s, mask_s, tri_s, bias_s = refs[-5:]
    bf = jnp.bfloat16
    row = lax.broadcasted_iota(jnp.int32, (R, D), 0)
    col = lax.broadcasted_iota(jnp.int32, (R, D), 1)

    @pl.when(pl.program_id(0) == 0)
    def _():
        tri_s[...] = jnp.where((col == 0) | (col > row), -BIG, 0.0).astype(bf)
        for t in range(2):
            for j in range(6):
                hot = (col == 0) & (row >= info[6 * t + j])
                if (t, j) in ((0, 0), (1, 5)):
                    hot = hot | ((col == row) & (col > 0))
                mask_s[t, j * R : (j + 1) * R, :] = jnp.where(hot, 1.0, 0.0).astype(bf)
                ok = row < info[6 * t + j]
                if (t, j) in ((0, 0), (1, 5)):
                    ok = ok & (row <= col)
                if (t, j) == (0, 5):
                    ok = ok & (row < 0)
                bias_s[j * R : (j + 1) * R, t * R : (t + 1) * R] = jnp.where(ok, 0.0, -BIG)

    k = jnp.concatenate([r[...] for r in k_refs], axis=0)
    v = jnp.concatenate([r[...] for r in v_refs], axis=0)
    qs, gs = [], []
    for t in range(2):
        live = row < info[12 + t]
        heads = [slice(h * D, (h + 1) * D) for h in range(GROUP)]
        rows = slice(t * R, (t + 1) * R)
        qs.append(jnp.concatenate([q_ref[rows, h] for h in heads], axis=0))
        gs.append(
            jnp.concatenate([jnp.where(live, g_ref[rows, h], jnp.zeros((), bf)) for h in heads], axis=0)
        )
    pair = 2 * R
    tri = jnp.concatenate([tri_s[...]] * 2, axis=0)
    sizes = (5 * R, 6 * R)
    k_wide = [jnp.concatenate([k[:n], mask_s[t, :n, :]], axis=1) for t, n in enumerate(sizes)]
    k_turned = k.T
    todo = [(t, h, sizes[t]) for t in range(2) for h in (0, 2)] + [(None, 4, 6 * R)]

    def rows_of(stacks, t, h):
        if t is None:
            return jnp.concatenate([one[h * R :] for one in stacks], axis=0)
        return stacks[t][h * R : (h + 2) * R]

    q_parts = [rows_of(qs, t, h) for t, h, _ in todo]
    g_parts = [rows_of(gs, t, h) for t, h, _ in todo]

    def products(step):
        t, _, n = todo[step]
        if t is None:
            s = dot(k, q_parts[step], 1, 1) + bias_s[...]
        else:
            s = dot(k_wide[t], jnp.concatenate([q_parts[step], tri], axis=1), 1, 1)
        return s, dot(v[:n], g_parts[step], 1, 1)

    def softmax_backward(step, s, dw):
        n, place = todo[step][2], slice(step * pair, (step + 1) * pair)
        m = jnp.max(s, axis=0, keepdims=True)
        e = jnp.exp2((s - m) * EXP2_SCALE)
        w = e * (1.0 / jnp.sum(e, axis=0, keepdims=True))
        delta = jnp.sum(w * dw, axis=0, keepdims=True)
        w_s[:n, place] = w.astype(bf)
        ds_s[:n, place] = (w * (dw - delta)).astype(bf)

    total = {}

    def gradients(step):
        t, h, n = todo[step]
        place = slice(step * pair, (step + 1) * pair)
        ds = ds_s[:n, place]
        for name, term in (
            (("k", n), dot(ds, q_parts[step], 1, 0)),
            (("v", n), dot(w_s[:n, place], g_parts[step], 1, 0)),
        ):
            total[name] = term if name not in total else total[name] + term
        dq = (dot(k_turned[:, :n], ds, 1, 0) * SCALE).T.astype(bf)
        for j in range(2):
            at, head = (j, h) if t is None else (t, h + j)
            dq_ref[at * R : (at + 1) * R, head * D : (head + 1) * D] = dq[j * R : (j + 1) * R]

    ahead = products(0)
    for step in range(len(todo)):
        now = ahead
        if step + 1 < len(todo):
            ahead = products(step + 1)
        if step:
            gradients(step - 1)
        softmax_backward(step, *now)
    gradients(len(todo) - 1)

    i = pl.program_id(0)
    n = 5 * R
    for name, at, scale in (("k", i, SCALE), ("v", count + i, 1.0)):
        cols = pl.ds(pl.multiple_of(at * D, D), D)
        inner, leaf = total[name, 5 * R], total[name, 6 * R]
        both = (inner + leaf[:n]) * scale
        for j in range(5):
            out_refs[j][:, cols] = both[j * R : (j + 1) * R].astype(out_refs[j].dtype)
        out_refs[5][:, cols] = (leaf[n:] * scale).astype(bf)


def attend_backward(info, q, g, k_slots, v_slots, first, count, grad_queries):
    specs = [pl.BlockSpec((2 * R, GROUP * D), lambda i, _: (0, first + i))] * 2
    arrays = [q, g]
    for array, block, offset in k_slots + v_slots:
        specs.append(pl.BlockSpec((R, D), functools.partial(lambda b, o, i, _: (b, o + i), block, offset)))
        arrays.append(array)
    kinds = [jnp.float32] + [jnp.bfloat16] * 5
    aliases = {}
    if grad_queries is not None:
        aliases = {1 + len(arrays): 0}
        specs.append(pl.BlockSpec(memory_space=pl.ANY))
        arrays.append(grad_queries)
    return pl.pallas_call(
        functools.partial(kernel, count),
        input_output_aliases=aliases,
        out_shape=[jax.ShapeDtypeStruct(q.shape, jnp.bfloat16)]
        + [jax.ShapeDtypeStruct((R, count * 2 * D), kind) for kind in kinds],
        grid_spec=pltpu.PrefetchScalarGridSpec(
            num_scalar_prefetch=1,
            grid=(count,),
            in_specs=specs,
            out_specs=[pl.BlockSpec((2 * R, GROUP * D), lambda i, _: (0, first + i))]
            + [pl.BlockSpec((R, count * 2 * D), lambda i, _: (0, 0))] * 6,
            scratch_shapes=[
                pltpu.VMEM((6 * R, 2 * GROUP * R), jnp.bfloat16),
                pltpu.VMEM((6 * R, 2 * GROUP * R), jnp.bfloat16),
                pltpu.VMEM((2, 6 * R, D), jnp.bfloat16),
                pltpu.VMEM((R, D), jnp.bfloat16),
                pltpu.VMEM((6 * R, 2 * R), jnp.float32),
            ],
        ),
        compiler_params=pltpu.CompilerParams(vmem_limit_bytes=50 * 2**20),
        cost_estimate=pl.CostEstimate(
            flops=count * 4_600_000_000, bytes_accessed=count * 2**20, transcendentals=count * 900_000
        ),
    )(info, *arrays)


def neighbours(x):
    swap = x ^ 1
    onward = jnp.where(x < 2, 2, 0)
    return swap, onward


def place_of(index):
    place = jnp.zeros_like(index)
    for bit in (3, 2, 1, 0):
        place = jnp.where((index >> bit) & 1 == 1, 4 - bit, place)
    return place


def shards(queries, keys, values, out_grad, seg_lengths):
    me = lax.axis_index("leaf")
    x, y = me & 3, me >> 2
    x_even, y_even = (x & 1) == 0, (y & 1) == 0
    x_swap, x_on = neighbours(x)
    y_swap, y_on = neighbours(y)
    ids = jnp.stack([me, 4 * y + x_swap, 4 * y + x_on, 4 * y_swap, 4 * y_on, me])
    lengths = jnp.take(seg_lengths[:, 0], ids).at[5].set(jnp.take(seg_lengths[:, 1], me))
    my_place = place_of(me)
    inner_limit = jnp.where((place_of(ids) < my_place) | (ids == me), lengths, 0)
    info = jnp.concatenate([inner_limit, lengths, lengths[:1], lengths[5:], jnp.zeros((2,), jnp.int32)])

    q = queries.reshape(2 * R, -1)
    g = out_grad.reshape(2 * R, -1)
    keys2, values2 = keys.reshape(2 * R, -1), values.reshape(2 * R, -1)

    f32, bf = jnp.float32, jnp.bfloat16
    firsts = [sum(CHUNKS[:c]) for c in range(len(CHUNKS))]
    sent, got, scored = {}, {}, {}

    def permute(value, axis, ring):
        return lax.ppermute(value, "leaf", pairs(axis, ring))

    def tie(value, after):
        return lax.optimization_barrier((value, tuple(after)))[0] if after else value

    def upper_of(c):
        return jnp.where(x == 0, sent[c], jnp.where(x == 1, got["a", c], got["b", c]))

    def move(name, c, after):
        if name == "g0":
            cols = slice(firsts[c] * D, (firsts[c] + CHUNKS[c]) * D)
            sent[c] = tie(jnp.concatenate([keys2[:R, cols], values2[:R, cols]], axis=1), after)
            got["a", c] = permute(sent[c], "x", SWAP)
            return [got["a", c]]
        if name == "g1":
            got["b", c] = permute(tie(jnp.where(x_even, sent[c], got["a", c]), after), "x", ONWARD)
            return [got["b", c]]
        if name == "g2":
            got["u", c] = tie(upper_of(c), after)
            got["c", c] = permute(got["u", c], "y", SWAP)
            return [got["c", c]]
        if name == "g3":
            got["d", c] = permute(tie(jnp.where(y_even, got["u", c], got["c", c]), after), "y", ONWARD)
            return [got["d", c]]
        own, a, b, near, far = scored[c][1:6]
        up = got.get(("up", c))
        if name == "r0":
            got[name, c] = permute(tie(far, after), "y", ONWARD).astype(f32)
        elif name == "r1":
            value = near.astype(f32) + jnp.where(y_even, 0.0, got["r0", c])
            got[name, c] = permute(tie(value.astype(bf), after), "y", SWAP).astype(f32)
            got["up", c] = jnp.where(y_even, got["r0", c], 0.0) + got[name, c]
        elif name == "r2":
            value = b.astype(f32) + jnp.where(x >= 2, up, 0.0)
            got[name, c] = permute(tie(value.astype(bf), after), "x", ONWARD).astype(f32)
        else:
            value = a.astype(f32) + jnp.where(x == 1, up, 0.0) + jnp.where(x_even, 0.0, got["r2", c])
            got[name, c] = permute(tie(value.astype(bf), after), "x", SWAP).astype(f32)
            total = own + jnp.where(x == 0, up, 0.0) + jnp.where(x_even, got["r2", c], 0.0)
            got["own", c] = (total + got[name, c]).astype(bf)
        back = [got[name, c]]
        return back

    def stage(moves, after):
        return [r for name, c in moves for r in move(name, c, after)]

    def score(c, after):
        k_slots = [(keys2, 0, firsts[c])] + [(got[n, c], 0, 0) for n in "abcd"] + [(keys2, 1, firsts[c])]
        v_slots = [(values2, 0, firsts[c])] + [(got[n, c], 0, CHUNKS[c]) for n in "abcd"]
        v_slots += [(values2, 1, firsts[c])]
        before = scored[c - 1][0] if c else None
        scored[c] = attend_backward(tie(info, after), q, g, k_slots, v_slots, firsts[c], CHUNKS[c], before)
        return list(scored[c][1:2])

    s1 = stage([("g0", 0)], [])
    s2 = stage([("g1", 0)], []) + stage([("g0", 1)], s1)
    s3 = stage([("g2", 0), ("g1", 1)], [])
    s4 = stage([("g3", 0), ("g2", 1)], [])
    k0 = score(0, s4)
    s5 = stage([("g3", 1)], [])
    s6 = stage([("r0", 0)], s5 + k0)
    k1 = score(1, s5 + k0)
    s7 = stage([("r0", 1), ("r1", 0)], s6 + k1)
    s8 = stage([("r1", 1), ("r2", 0)], [])
    s9 = stage([("r2", 1), ("r3", 0)], [])
    stage([("r3", 1)], [])

    grad_queries = scored[len(CHUNKS) - 1][0]
    inner = [got["own", c] for c in range(len(CHUNKS))]
    leaf = [scored[c][6] for c in range(len(CHUNKS))]

    def assemble(half):
        rows = []
        for pieces in (inner, leaf):
            cut = [p[:, half * c * D : (half + 1) * c * D] for p, c in zip(pieces, CHUNKS)]
            rows.append(jnp.concatenate(cut, axis=1))
        return jnp.stack(rows)[None]

    return grad_queries.reshape(queries.shape), assemble(0), assemble(1)


def solution(mesh):
    rows = P(("prompt", "leaf"), None, None, None)
    return jax.shard_map(
        shards,
        mesh=mesh,
        in_specs=(rows, rows, rows, rows, P("prompt", None)),
        out_specs=(rows, rows, rows),
        check_vma=False,
    )
```
